32 devices in a mesh: stn: 16 (over z, x, core), elem: 2 (over y).
Axes of the slice: x: 2, y: 2, z: 4, core: 2. Of those that a mesh axis runs over, the one named last changes fastest.
Arguments:
- voltages: bfloat16 [2, 16, 64, 16, 128], P(None, 'stn', 'elem'), may hold values from -6 to 6
- weights: bfloat16 [2, 8, 64, 16], P(None, None, 'elem'), may hold values from -0.5 to 0.5
Outputs:
- spectra: float32 [2, 16, 128, 128], P(None, 'elem', 'stn')
The draws below stay inside these ranges and needn't reach their ends.
All inputs are finite; a program needn't handle non-finite values.
Results may differ from the reference program's by a relative error of at most 0.0075.
Values may be sent and summed in bfloat16 or wider, within the bound.
No kernel may reach another device: no remote copies, remote signals or barrier semaphores. Data moves between devices by JAX's collectives and lax.ppermute only.
A program may use at most 64 MiB of HBM per device.

```python
import jax
import jax.numpy as jnp
from jax import lax

ELEMS = 64
NB = 8
CH = 16
T_SIZE = 128
STATIONS = 16
BEAMS = 128


def level_of(rng, shape, cuts, least, high):
    def one(position, parts):
        heights = jax.random.uniform(jax.random.fold_in(jax.random.fold_in(rng, 6), position), (parts,), jnp.float32, least / len(cuts), high / len(cuts))
        return jnp.repeat(jnp.exp(heights), shape[position] // parts).reshape((-1,) + (1,) * (len(shape) - position - 1))

    gain = one(*cuts[0])
    for cut in cuts[1:]:
        gain = gain * one(*cut)
    return gain


def centred(stream_key, dims, scale, bound, shards=(), held_as=jnp.bfloat16):
    drawn = scale * jax.random.normal(stream_key, dims, jnp.float32)
    if shards:
        drawn = drawn * level_of(stream_key, dims, shards, -0.22, 0.18)
    return jnp.clip(drawn, -bound, bound).astype(held_as)


def setup_inputs(seed: int = 0) -> dict:
    streams_of = jax.random.split(jax.random.key(seed), 3)
    voltages = centred(streams_of[0], (2, STATIONS, ELEMS, CH, T_SIZE), 1.0, 6.0, ((1, 16), (2, 2)))
    weights = centred(streams_of[1], (2, NB, ELEMS, CH), (2 * ELEMS) ** -0.5, 0.5, ((2, 2),))
    return dict(voltages=voltages, weights=weights)


def reference(voltages, weights):
    volt_real = voltages[0].astype(jnp.float32)
    volt_imag = voltages[1].astype(jnp.float32)
    weight_real = weights[0].astype(jnp.float32)
    weight_imag = weights[1].astype(jnp.float32)
    beam_real = jnp.einsum("kec,sect->sckt", weight_real, volt_real) + jnp.einsum("kec,sect->sckt", weight_imag, volt_imag)
    beam_imag = jnp.einsum("kec,sect->sckt", weight_real, volt_imag) - jnp.einsum("kec,sect->sckt", weight_imag, volt_real)
    stacked = jnp.stack([beam_real, beam_imag]).astype(jnp.bfloat16)
    stacked = jnp.transpose(stacked, (0, 2, 1, 3, 4)).reshape(2, CH, BEAMS, T_SIZE)

    def one_channel(pair):
        left_real, left_imag = pair
        spec_real = jnp.dot(left_real, left_real.T, preferred_element_type=jnp.float32) + jnp.dot(left_imag, left_imag.T, preferred_element_type=jnp.float32)
        spec_imag = jnp.dot(left_imag, left_real.T, preferred_element_type=jnp.float32) - jnp.dot(left_real, left_imag.T, preferred_element_type=jnp.float32)
        return jnp.stack([spec_real, spec_imag]) / jnp.float32(T_SIZE)

    result = lax.map(one_channel, (stacked[0], stacked[1]))
    return jnp.transpose(result, (1, 0, 2, 3))
```

```python
import functools

import jax
import jax.numpy as jnp
from jax import lax
from jax.experimental import pallas as pl
from jax.experimental.pallas import tpu as pltpu
from jax.sharding import PartitionSpec as P


def beam_kernel(parts, v_ref, w_ref, mine_ref, send_ref, w32, both):
    planes, elems, chans, samples = v_ref.shape
    rows = w_ref.shape[0] // chans
    deep = elems * chans
    w32[...] = w_ref[...].astype(jnp.float32)
    by_channel = jnp.concatenate([w32[pl.ds(c, rows, stride=chans), :] for c in range(chans)])
    lane = lax.broadcasted_iota(jnp.int32, (elems, deep), 1)
    low = lax.broadcasted_iota(jnp.int32, (elems, deep), 0) * chans
    spread = jnp.where((lane >= low) & (lane < low + chans), 1.0, 0.0).astype(jnp.bfloat16)
    wide = jnp.dot(by_channel.astype(jnp.bfloat16), spread, preferred_element_type=jnp.float32)
    wide = wide.reshape(chans, rows, deep)
    lane = lax.rem(lax.broadcasted_iota(jnp.int32, wide.shape, 2), chans)
    wide = jnp.where(lane == lax.broadcasted_iota(jnp.int32, wide.shape, 0), wide, 0.0)
    wide = wide.reshape(chans * rows, deep).astype(jnp.bfloat16)
    volts = v_ref[...].reshape(planes, deep, samples)
    half = rows // 2
    by_real = jnp.dot(wide, volts[0], preferred_element_type=jnp.float32).reshape(chans, 2, half, samples)
    by_imag = jnp.dot(wide, volts[1], preferred_element_type=jnp.float32).reshape(chans, 2, half, samples)
    both[:, 0] = by_real[:, 0] + by_imag[:, 1]
    both[:, 1] = by_imag[:, 0] - by_real[:, 1]
    owned = chans // parts
    me = lax.axis_index("elem")
    mine_ref[...] = both[pl.ds(me * owned, owned)].reshape(mine_ref.shape)
    for step in range(1, parts):
        other = lax.rem(me + step, parts) * owned
        send_ref[step - 1] = both[pl.ds(other, owned)].reshape(mine_ref.shape).astype(jnp.bfloat16)


def partial_beams(voltages, weights, parts):
    planes, _, elems, chans, samples = voltages.shape
    rows = planes * weights.shape[1]
    owned = chans // parts
    return pl.pallas_call(
        functools.partial(beam_kernel, parts),
        out_shape=(
            jax.ShapeDtypeStruct((owned, rows, samples), jnp.float32),
            jax.ShapeDtypeStruct((parts - 1, owned, rows, samples), jnp.bfloat16),
        ),
        scratch_shapes=[
            pltpu.VMEM((rows * chans, elems), jnp.float32),
            pltpu.VMEM((chans, planes, rows // planes, samples), jnp.float32),
        ],
    )(voltages[:, 0], weights.transpose(0, 1, 3, 2).reshape(rows * chans, elems))


def spectra_kernel(order, *refs):
    blocks, out_ref = refs[:-1], refs[-1]
    chans, rows, samples = blocks[0].shape[1:]
    half = rows // 2
    where = [(ref, i) for ref in blocks for i in range(ref.shape[0])]
    me = lax.axis_index("stn")
    found = []
    for c in range(chans):
        tiles = [where[k][0][where[k][1], c].astype(jnp.float32) for k in order]
        real = jnp.concatenate([t[:half] for t in tiles]).astype(jnp.bfloat16)
        imag = jnp.concatenate([t[half:] for t in tiles]).astype(jnp.bfloat16)
        own = tiles[0]
        left = jnp.concatenate([own, jnp.concatenate([own[half:], -own[:half]])], axis=1)
        right = jnp.concatenate([real, imag], axis=1)
        found.append(
            lax.dot_general(
                left.astype(jnp.bfloat16), right, (((1,), (1,)), ((), ())),
                preferred_element_type=jnp.float32,
            )
        )
    spec = jnp.concatenate(found)
    beams = spec.shape[1]
    lane = lax.broadcasted_iota(jnp.int32, spec.shape, 1)
    bit, width = 1, half
    while width < beams:
        if width < 128:
            moved = jnp.where(
                lane & width == 0, pltpu.roll(spec, beams - width, 1), pltpu.roll(spec, width, 1)
            )
        else:
            cuts = [spec[:, at : at + width] for at in range(0, beams, width)]
            moved = jnp.concatenate([cuts[i ^ 1] for i in range(len(cuts))], axis=1)
        spec = jnp.where(me & bit != 0, moved, spec)
        bit, width = bit * 2, width * 2
    spec = spec.reshape(chans, 2, half, beams) / jnp.float32(samples)
    out_ref[0] = spec[:, 0]
    out_ref[1] = spec[:, 1]


def cross_spectra(blocks, offsets):
    chans, rows, samples = blocks[0].shape[1:]
    stations = len(offsets)
    order = [offsets.index(d) for d in range(stations)]
    return pl.pallas_call(
        functools.partial(spectra_kernel, order),
        out_shape=jax.ShapeDtypeStruct((2, chans, rows // 2, stations * (rows // 2)), jnp.float32),
    )(*blocks)


def body(steps, stations, parts, voltages, weights):
    mine, sent = partial_beams(voltages, weights, parts)
    for step in range(1, parts):
        pairs = [(i, (i + step) % parts) for i in range(parts)]
        mine = mine + lax.ppermute(sent[step - 1], "elem", pairs).astype(jnp.float32)
    held = mine.astype(jnp.bfloat16)[None]
    offsets = [0]
    for step in steps[:-1]:
        got = lax.ppermute(held, "stn", [(i, i ^ step) for i in range(stations)])
        held = jnp.concatenate([held, got])
        offsets += [o ^ step for o in offsets]
    step = steps[-1]
    got = lax.ppermute(held, "stn", [(i, i ^ step) for i in range(stations)])
    offsets += [o ^ step for o in offsets]
    return cross_spectra([held, got], offsets)


def solution(mesh):
    stations, parts = mesh.shape["stn"], mesh.shape["elem"]
    steps = []
    bit = stations // 2
    while bit > 1:
        steps.append(bit + 1)
        bit //= 2
    steps.append(1)
    placed = (P(None, "stn", "elem", None, None), P(None, None, "elem", None))
    return jax.shard_map(
        functools.partial(body, steps, stations, parts),
        mesh=mesh, in_specs=placed, out_specs=P(None, "elem", "stn", None), check_vma=False,
    )
```

```python
import functools

import jax
import jax.numpy as jnp
from jax import lax
from jax.experimental import pallas as pl
from jax.experimental.pallas import tpu as pltpu
from jax.sharding import PartitionSpec as P


def room_for(*arrays):
    return (4 << 20) + 4 * sum(a.size * a.dtype.itemsize for a in arrays)


def beam_kernel(parts, v_ref, w_ref, mine_ref, copy_ref, send_ref, w16, w32, volts, both, sems):
    planes, elems, chans, samples = v_ref.shape
    rows = w_ref.shape[0] // chans
    deep = elems * chans
    loads = [pltpu.make_async_copy(w_ref, w16, sems.at[planes])]
    loads += [pltpu.make_async_copy(v_ref.at[p], volts.at[p], sems.at[p]) for p in range(planes)]
    for load in loads:
        load.start()
    lane = lax.broadcasted_iota(jnp.int32, (elems, deep), 1)
    low = lax.broadcasted_iota(jnp.int32, (elems, deep), 0) * chans
    spread = jnp.where((lane >= low) & (lane < low + chans), 1.0, 0.0).astype(jnp.bfloat16)
    loads[0].wait()
    w32[...] = w16[...].astype(jnp.float32)
    by_channel = jnp.concatenate([w32[pl.ds(c, rows, stride=chans), :] for c in range(chans)])
    wide = jnp.dot(by_channel.astype(jnp.bfloat16), spread, preferred_element_type=jnp.float32)
    wide = wide.reshape(chans, rows, deep)
    lane = lax.rem(lax.broadcasted_iota(jnp.int32, wide.shape, 2), chans)
    wide = jnp.where(lane == lax.broadcasted_iota(jnp.int32, wide.shape, 0), wide, 0.0)
    wide = wide.reshape(chans * rows, deep).astype(jnp.bfloat16)
    half = rows // 2
    loads[1].wait()
    by_real = jnp.dot(wide, volts[0].reshape(deep, samples), preferred_element_type=jnp.float32)
    by_real = by_real.reshape(chans, 2, half, samples)
    loads[2].wait()
    by_imag = jnp.dot(wide, volts[1].reshape(deep, samples), preferred_element_type=jnp.float32)
    by_imag = by_imag.reshape(chans, 2, half, samples)
    both[:, 0] = by_real[:, 0] + by_imag[:, 1]
    both[:, 1] = by_imag[:, 0] - by_real[:, 1]
    owned = chans // parts
    me = lax.axis_index("elem")
    mine_ref[...] = both[pl.ds(me * owned, owned)].reshape(mine_ref.shape)
    copy_ref[...] = mine_ref[...].astype(jnp.bfloat16)
    for step in range(1, parts):
        other = lax.rem(me + step, parts) * owned
        send_ref[step - 1] = both[pl.ds(other, owned)].reshape(mine_ref.shape).astype(jnp.bfloat16)


def partial_beams(voltages, weights, parts):
    planes, _, elems, chans, samples = voltages.shape
    rows = planes * weights.shape[1]
    owned = chans // parts
    return pl.pallas_call(
        functools.partial(beam_kernel, parts),
        in_specs=[pl.BlockSpec(memory_space=pltpu.HBM)] * 2,
        out_shape=(
            jax.ShapeDtypeStruct((owned, rows, samples), jnp.float32),
            jax.ShapeDtypeStruct((owned, rows, samples), jnp.bfloat16),
            jax.ShapeDtypeStruct((parts - 1, owned, rows, samples), jnp.bfloat16),
        ),
        out_specs=[pl.BlockSpec(memory_space=pltpu.VMEM)] * 3,
        compiler_params=pltpu.CompilerParams(vmem_limit_bytes=55080 << 10),
        scratch_shapes=[
            pltpu.VMEM((rows * chans, elems), weights.dtype),
            pltpu.VMEM((rows * chans, elems), jnp.float32),
            pltpu.VMEM((planes, elems, chans, samples), voltages.dtype),
            pltpu.VMEM((chans, planes, rows // planes, samples), jnp.float32),
            pltpu.SemaphoreType.DMA((planes + 1,)),
        ],
    )(voltages[:, 0], weights.transpose(0, 1, 3, 2).reshape(rows * chans, elems))


def spectra_kernel(order, *refs):
    blocks, out_ref = refs[:-1], refs[-1]
    chans, rows, samples = blocks[0].shape[1:]
    half = rows // 2
    where = [(ref, i) for ref in blocks for i in range(ref.shape[0])]
    me = lax.axis_index("stn")
    found = []
    for c in range(chans):
        tiles = [where[k][0][where[k][1], c].astype(jnp.float32) for k in order]
        real = jnp.concatenate([t[:half] for t in tiles]).astype(jnp.bfloat16)
        imag = jnp.concatenate([t[half:] for t in tiles]).astype(jnp.bfloat16)
        own = tiles[0]
        left = jnp.concatenate([own, jnp.concatenate([own[half:], -own[:half]])], axis=1)
        right = jnp.concatenate([real, imag], axis=1)
        found.append(
            lax.dot_general(
                left.astype(jnp.bfloat16), right, (((1,), (1,)), ((), ())),
                preferred_element_type=jnp.float32,
            )
        )
    spec = jnp.concatenate(found)
    beams = spec.shape[1]
    lane = lax.broadcasted_iota(jnp.int32, spec.shape, 1)
    bit, width = 1, half
    while width < beams:
        if width < 128:
            moved = jnp.where(
                lane & width == 0, pltpu.roll(spec, beams - width, 1), pltpu.roll(spec, width, 1)
            )
        else:
            cuts = [spec[:, at : at + width] for at in range(0, beams, width)]
            moved = jnp.concatenate([cuts[i ^ 1] for i in range(len(cuts))], axis=1)
        spec = jnp.where(me & bit != 0, moved, spec)
        bit, width = bit * 2, width * 2
    spec = spec.reshape(chans, 2, half, beams) / jnp.float32(samples)
    out_ref[0] = spec[:, 0]
    out_ref[1] = spec[:, 1]


def cross_spectra(blocks, offsets):
    chans, rows, samples = blocks[0].shape[1:]
    stations = len(offsets)
    order = [offsets.index(d) for d in range(stations)]
    return pl.pallas_call(
        functools.partial(spectra_kernel, order),
        out_shape=jax.ShapeDtypeStruct((2, chans, rows // 2, stations * (rows // 2)), jnp.float32),
        compiler_params=pltpu.CompilerParams(vmem_limit_bytes=room_for(*blocks)),
    )(*blocks)


def gather_plan(stations):
    bits = []
    while stations > 2:
        stations //= 2
        bits.append(stations)
    first, rest = bits[0], bits[1:]
    stages = []
    while rest:
        pair, rest = rest[:2], rest[2:]
        stages.append([b + 1 for b in pair] + ([sum(pair) + 1] if len(pair) == 2 else []))
    return first + 1, stages + [[1]]


def body(stations, parts, voltages, weights):
    mine, copy, sent = partial_beams(voltages, weights, parts)
    near, stages = gather_plan(stations)
    other = lax.ppermute(copy, "stn", [(i, i ^ near) for i in range(stations)]).astype(jnp.float32)
    for step in range(1, parts):
        here = [(e, (e + step) % parts) for e in range(parts)]
        there = [(s * parts + e, (s ^ near) * parts + f) for s in range(stations) for e, f in here]
        mine = mine + lax.ppermute(sent[step - 1], "elem", here).astype(jnp.float32)
        other = other + lax.ppermute(sent[step - 1], ("stn", "elem"), there).astype(jnp.float32)
    held, offsets = jnp.stack([mine, other]).astype(jnp.bfloat16), [0, near]
    for steps in stages:
        got = [lax.ppermute(held, "stn", [(i, i ^ step) for i in range(stations)]) for step in steps]
        offsets = offsets + [o ^ step for step in steps for o in offsets]
        if steps is not stages[-1]:
            held = jnp.concatenate([held] + got)
    return cross_spectra([held] + got, offsets)


def solution(mesh):
    placed = (P(None, "stn", "elem", None, None), P(None, None, "elem", None))
    return jax.shard_map(
        functools.partial(body, mesh.shape["stn"], mesh.shape["elem"]),
        mesh=mesh, in_specs=placed, out_specs=P(None, "elem", "stn", None), check_vma=False,
    )
```

```python
import functools

import jax
import jax.numpy as jnp
from jax import lax
from jax.experimental import pallas as pl
from jax.experimental.pallas import tpu as pltpu
from jax.sharding import PartitionSpec as P


def room_for(*arrays):
    return (4 << 20) + 4 * sum(a.size * a.dtype.itemsize for a in arrays)


def beam_kernel(parts, v_ref, w_ref, mine_ref, copy_ref, send_ref, w16, w32, volts, both, sems):
    planes, elems, chans, samples = v_ref.shape
    rows = w_ref.shape[0] // chans
    deep = elems * chans
    loads = [pltpu.make_async_copy(w_ref, w16, sems.at[planes])]
    loads += [pltpu.make_async_copy(v_ref.at[p], volts.at[p], sems.at[p]) for p in range(planes)]
    for load in loads:
        load.start()
    lane = lax.broadcasted_iota(jnp.int32, (elems, deep), 1)
    low = lax.broadcasted_iota(jnp.int32, (elems, deep), 0) * chans
    spread = jnp.where((lane >= low) & (lane < low + chans), 1.0, 0.0).astype(jnp.bfloat16)
    loads[0].wait()
    w32[...] = w16[...].astype(jnp.float32)
    by_channel = jnp.concatenate([w32[pl.ds(c, rows, stride=chans), :] for c in range(chans)])
    wide = jnp.dot(by_channel.astype(jnp.bfloat16), spread, preferred_element_type=jnp.float32)
    wide = wide.reshape(chans, rows, deep)
    lane = lax.rem(lax.broadcasted_iota(jnp.int32, wide.shape, 2), chans)
    wide = jnp.where(lane == lax.broadcasted_iota(jnp.int32, wide.shape, 0), wide, 0.0)
    wide = wide.reshape(chans * rows, deep).astype(jnp.bfloat16)
    half = rows // 2
    loads[1].wait()
    by_real = jnp.dot(wide, volts[0].reshape(deep, samples), preferred_element_type=jnp.float32)
    by_real = by_real.reshape(chans, 2, half, samples)
    loads[2].wait()
    by_imag = jnp.dot(wide, volts[1].reshape(deep, samples), preferred_element_type=jnp.float32)
    by_imag = by_imag.reshape(chans, 2, half, samples)
    both[:, 0] = by_real[:, 0] + by_imag[:, 1]
    both[:, 1] = by_imag[:, 0] - by_real[:, 1]
    owned = chans // parts
    me = lax.axis_index("elem")
    mine_ref[...] = both[pl.ds(me * owned, owned)].reshape(mine_ref.shape)
    copy_ref[...] = mine_ref[...].astype(jnp.bfloat16)
    for step in range(1, parts):
        other = lax.rem(me + step, parts) * owned
        send_ref[step - 1] = both[pl.ds(other, owned)].reshape(mine_ref.shape).astype(jnp.bfloat16)


def partial_beams(voltages, weights, parts):
    planes, _, elems, chans, samples = voltages.shape
    rows = planes * weights.shape[1]
    owned = chans // parts
    return pl.pallas_call(
        functools.partial(beam_kernel, parts),
        in_specs=[pl.BlockSpec(memory_space=pltpu.HBM)] * 2,
        out_shape=(
            jax.ShapeDtypeStruct((owned, rows, samples), jnp.float32),
            jax.ShapeDtypeStruct((owned, rows, samples), jnp.bfloat16),
            jax.ShapeDtypeStruct((parts - 1, owned, rows, samples), jnp.bfloat16),
        ),
        out_specs=[pl.BlockSpec(memory_space=pltpu.VMEM)] * 3,
        compiler_params=pltpu.CompilerParams(vmem_limit_bytes=55080 << 10),
        scratch_shapes=[
            pltpu.VMEM((rows * chans, elems), weights.dtype),
            pltpu.VMEM((rows * chans, elems), jnp.float32),
            pltpu.VMEM((planes, elems, chans, samples), voltages.dtype),
            pltpu.VMEM((chans, planes, rows // planes, samples), jnp.float32),
            pltpu.SemaphoreType.DMA((planes + 1,)),
        ],
    )(voltages[:, 0], weights.transpose(0, 1, 3, 2).reshape(rows * chans, elems))


def place_of(chip, stages):
    index, flip, size = 0, 0, 1
    for steps in stages:
        bits = [s >> 1 for s in steps if (s >> 1) & ((s >> 1) - 1) == 0]
        spots, flips = 0, 0
        for at, step in enumerate(steps):
            key = sum(1 << j for j, b in enumerate(bits) if (step >> 1) & b)
            spots |= (at + 1) << (2 * key)
            flips |= (step & 1) << key
        key = sum(((chip >> (b.bit_length() - 1)) & 1) << j for j, b in enumerate(bits))
        index = index + ((spots >> (2 * key)) & 3) * size
        flip = flip ^ ((flips >> key) & 1)
        size *= len(steps) + 1
    return index, flip


def spectra_kernel(stages, held_ref, got_ref, out_ref):
    chips, chans, rows, samples = held_ref.shape
    half = rows // 2
    me = lax.axis_index("stn")
    places = []
    for chip in range(chips):
        index, flip = place_of((me >> 1) ^ chip, stages)
        places.append((index, ((me & 1) ^ flip) == 0))
    found = []
    for c in range(chans):
        tiles = []
        for index, held_first in places:
            held, got = held_ref[index, c], got_ref[index, c]
            tiles += [jnp.where(held_first, held, got), jnp.where(held_first, got, held)]
        tiles = [t.astype(jnp.float32) for t in tiles]
        real = jnp.concatenate([t[:half] for t in tiles])
        imag = jnp.concatenate([t[half:] for t in tiles])
        own = held_ref[0, c].astype(jnp.float32)
        left = jnp.concatenate([own, jnp.concatenate([own[half:], -own[:half]])], axis=1)
        right = jnp.concatenate([real, imag], axis=1)
        found.append(
            lax.dot_general(
                left.astype(jnp.bfloat16), right.astype(jnp.bfloat16), (((1,), (1,)), ((), ())),
                preferred_element_type=jnp.float32,
            )
        )
    spec = jnp.concatenate(found).reshape(chans, 2, half, -1) / jnp.float32(samples)
    out_ref[0] = spec[:, 0]
    out_ref[1] = spec[:, 1]


def cross_spectra(held, got, stages):
    chips, chans, rows, samples = held.shape
    half = rows // 2
    return pl.pallas_call(
        functools.partial(spectra_kernel, stages),
        out_shape=jax.ShapeDtypeStruct((2, chans, half, 2 * chips * half), jnp.float32),
        compiler_params=pltpu.CompilerParams(vmem_limit_bytes=room_for(held, got)),
    )(held, got)


def gather_plan(stations):
    bits = []
    while stations > 2:
        stations //= 2
        bits.append(stations)
    first, rest = bits[0], bits[1:]
    stages = []
    while rest:
        pair, rest = rest[:2], rest[2:]
        stages.append([sum(pair), pair[0], pair[1] + 1] if len(pair) == 2 else [pair[0] + 1])
    return first + 1, stages


def body(stations, parts, voltages, weights):
    mine, copy, sent = partial_beams(voltages, weights, parts)
    near, stages = gather_plan(stations)
    other = lax.ppermute(copy, "stn", [(i, i ^ near) for i in range(stations)]).astype(jnp.float32)
    for step in range(1, parts):
        here = [(e, (e + step) % parts) for e in range(parts)]
        there = [(s * parts + e, (s ^ near) * parts + f) for s in range(stations) for e, f in here]
        mine = mine + lax.ppermute(sent[step - 1], "elem", here).astype(jnp.float32)
        other = other + lax.ppermute(sent[step - 1], ("stn", "elem"), there).astype(jnp.float32)
    held = jnp.stack([mine, other]).astype(jnp.bfloat16)
    for steps in stages:
        got = [lax.ppermute(held, "stn", [(i, i ^ step) for i in range(stations)]) for step in steps]
        held = jnp.concatenate([held] + got)
    got = lax.ppermute(held, "stn", [(i, i ^ 1) for i in range(stations)])
    return cross_spectra(held, got, [[near]] + stages)


def solution(mesh):
    placed = (P(None, "stn", "elem", None, None), P(None, None, "elem", None))
    return jax.shard_map(
        functools.partial(body, mesh.shape["stn"], mesh.shape["elem"]),
        mesh=mesh, in_specs=placed, out_specs=P(None, "elem", "stn", None), check_vma=False,
    )
```

```python
import functools

import jax
import jax.numpy as jnp
from jax import lax
from jax.experimental import pallas as pl
from jax.experimental.pallas import tpu as pltpu
from jax.sharding import PartitionSpec as P


def room_for(*arrays):
    return (4 << 20) + 4 * sum(a.size * a.dtype.itemsize for a in arrays)


def beam_kernel(parts, v_ref, w_ref, mine_ref, copy_ref, send_ref, w16, w32, volts, both, sems):
    planes, elems, chans, samples = v_ref.shape
    rows = w_ref.shape[0] // chans
    deep = elems * chans
    loads = [
        pltpu.make_async_copy(w_ref, w16, sems.at[0]), pltpu.make_async_copy(v_ref, volts, sems.at[1])
    ]
    for load in loads:
        load.start()
    lane = lax.broadcasted_iota(jnp.int32, (elems, deep), 1)
    low = lax.broadcasted_iota(jnp.int32, (elems, deep), 0) * chans
    spread = jnp.where((lane >= low) & (lane < low + chans), 1.0, 0.0).astype(jnp.bfloat16)
    loads[0].wait()
    w32[...] = w16[...].astype(jnp.float32)
    by_channel = jnp.concatenate([w32[pl.ds(c, rows, stride=chans), :] for c in range(chans)])
    wide = jnp.dot(by_channel.astype(jnp.bfloat16), spread, preferred_element_type=jnp.float32)
    wide = wide.reshape(chans, rows, deep)
    lane = lax.rem(lax.broadcasted_iota(jnp.int32, wide.shape, 2), chans)
    wide = jnp.where(lane == lax.broadcasted_iota(jnp.int32, wide.shape, 0), wide, 0.0)
    wide = wide.reshape(chans * rows, deep).astype(jnp.bfloat16)
    half = rows // 2
    loads[1].wait()
    volts_both = jnp.concatenate([volts[p].reshape(deep, samples) for p in range(planes)], axis=1)
    sums = jnp.dot(wide, volts_both, preferred_element_type=jnp.float32)
    sums = sums.reshape(chans, 2, half, planes * samples)
    by_real, by_imag = sums[..., :samples], sums[..., samples:]
    both[:, 0] = by_real[:, 0] + by_imag[:, 1]
    both[:, 1] = by_imag[:, 0] - by_real[:, 1]
    owned = chans // parts
    me = lax.axis_index("elem")
    mine_ref[...] = both[pl.ds(me * owned, owned)].reshape(mine_ref.shape)
    copy_ref[...] = mine_ref[...].astype(jnp.bfloat16)
    for step in range(1, parts):
        other = lax.rem(me + step, parts) * owned
        send_ref[step - 1] = both[pl.ds(other, owned)].reshape(mine_ref.shape).astype(jnp.bfloat16)


def partial_beams(voltages, weights, parts):
    planes, _, elems, chans, samples = voltages.shape
    rows = planes * weights.shape[1]
    owned = chans // parts
    return pl.pallas_call(
        functools.partial(beam_kernel, parts),
        in_specs=[pl.BlockSpec(memory_space=pltpu.HBM)] * 2,
        out_shape=(
            jax.ShapeDtypeStruct((owned, rows, samples), jnp.float32),
            jax.ShapeDtypeStruct((owned, rows, samples), jnp.bfloat16),
            jax.ShapeDtypeStruct((parts - 1, owned, rows, samples), jnp.bfloat16),
        ),
        out_specs=[pl.BlockSpec(memory_space=pltpu.VMEM)] * 3,
        compiler_params=pltpu.CompilerParams(vmem_limit_bytes=55080 << 10),
        scratch_shapes=[
            pltpu.VMEM((rows * chans, elems), weights.dtype),
            pltpu.VMEM((rows * chans, elems), jnp.float32),
            pltpu.VMEM((planes, elems, chans, samples), voltages.dtype),
            pltpu.VMEM((chans, planes, rows // planes, samples), jnp.float32),
            pltpu.SemaphoreType.DMA((2,)),
        ],
    )(voltages[:, 0], weights.transpose(0, 1, 3, 2).reshape(rows * chans, elems))


def place_of(chip, stages):
    index, flip, size = 0, 0, 1
    for steps in stages:
        bits = [s >> 1 for s in steps if (s >> 1) & ((s >> 1) - 1) == 0]
        spots, flips = 0, 0
        for at, step in enumerate(steps):
            key = sum(1 << j for j, b in enumerate(bits) if (step >> 1) & b)
            spots |= (at + 1) << (2 * key)
            flips |= (step & 1) << key
        key = sum(((chip >> (b.bit_length() - 1)) & 1) << j for j, b in enumerate(bits))
        index = index + ((spots >> (2 * key)) & 3) * size
        flip = flip ^ ((flips >> key) & 1)
        size *= len(steps) + 1
    return index, flip


def spectra_kernel(stages, held_ref, got_ref, out_ref):
    chips, chans, rows, samples = held_ref.shape
    half = rows // 2
    me = lax.axis_index("stn")
    places = []
    for chip in range(chips):
        index, flip = place_of((me >> 1) ^ chip, stages)
        places.append((index, ((me & 1) ^ flip) == 0))
    found = []
    for c in range(chans):
        tiles = []
        for index, held_first in places:
            held, got = held_ref[index, c], got_ref[index, c]
            tiles += [jnp.where(held_first, held, got), jnp.where(held_first, got, held)]
        tiles = [t.astype(jnp.float32) for t in tiles]
        real = jnp.concatenate([t[:half] for t in tiles])
        imag = jnp.concatenate([t[half:] for t in tiles])
        own = held_ref[0, c].astype(jnp.float32)
        left = jnp.concatenate([own, jnp.concatenate([own[half:], -own[:half]])], axis=1)
        right = jnp.concatenate([real, imag], axis=1)
        found.append(
            lax.dot_general(
                left.astype(jnp.bfloat16), right.astype(jnp.bfloat16), (((1,), (1,)), ((), ())),
                preferred_element_type=jnp.float32,
            )
        )
    spec = jnp.concatenate(found).reshape(chans, 2, half, -1) / jnp.float32(samples)
    out_ref[0] = spec[:, 0]
    out_ref[1] = spec[:, 1]


def cross_spectra(held, got, stages):
    chips, chans, rows, samples = held.shape
    half = rows // 2
    return pl.pallas_call(
        functools.partial(spectra_kernel, stages),
        out_shape=jax.ShapeDtypeStruct((2, chans, half, 2 * chips * half), jnp.float32),
        compiler_params=pltpu.CompilerParams(vmem_limit_bytes=room_for(held, got)),
    )(held, got)


def gather_plan(stations):
    bits = []
    while stations > 2:
        stations //= 2
        bits.append(stations)
    first, rest = bits[0], bits[1:]
    stages = []
    while rest:
        pair, rest = rest[:2], rest[2:]
        stages.append([sum(pair), pair[0], pair[1] + 1] if len(pair) == 2 else [pair[0] + 1])
    return first + 1, stages


def body(stations, parts, voltages, weights):
    mine, copy, sent = partial_beams(voltages, weights, parts)
    near, stages = gather_plan(stations)
    other = lax.ppermute(copy, "stn", [(i, i ^ near) for i in range(stations)]).astype(jnp.float32)
    for step in range(1, parts):
        here = [(e, (e + step) % parts) for e in range(parts)]
        there = [(s * parts + e, (s ^ near) * parts + f) for s in range(stations) for e, f in here]
        mine = mine + lax.ppermute(sent[step - 1], "elem", here).astype(jnp.float32)
        other = other + lax.ppermute(sent[step - 1], ("stn", "elem"), there).astype(jnp.float32)
    held = jnp.stack([mine, other]).astype(jnp.bfloat16)
    for steps in stages:
        got = [lax.ppermute(held, "stn", [(i, i ^ step) for i in range(stations)]) for step in steps]
        held = jnp.concatenate([held] + got)
    got = lax.ppermute(held, "stn", [(i, i ^ 1) for i in range(stations)])
    return cross_spectra(held, got, [[near]] + stages)


def solution(mesh):
    placed = (P(None, "stn", "elem", None, None), P(None, None, "elem", None))
    return jax.shard_map(
        functools.partial(body, mesh.shape["stn"], mesh.shape["elem"]),
        mesh=mesh, in_specs=placed, out_specs=P(None, "elem", "stn", None), check_vma=False,
    )
```

```python
import functools

import jax
import jax.numpy as jnp
from jax import lax
from jax.experimental import pallas as pl
from jax.experimental.pallas import tpu as pltpu
from jax.sharding import PartitionSpec as P


def room_for(*arrays):
    return (4 << 20) + 4 * sum(a.size * a.dtype.itemsize for a in arrays)


def beam_kernel(parts, v_ref, w_ref, mine_ref, copy_ref, send_ref, w16, w32, volts, both, sems):
    planes, elems, chans, samples = v_ref.shape
    rows = w_ref.shape[0] // chans
    deep = elems * chans
    loads = [
        pltpu.make_async_copy(w_ref, w16, sems.at[0]), pltpu.make_async_copy(v_ref, volts, sems.at[1])
    ]
    for load in loads:
        load.start()
    lane = lax.broadcasted_iota(jnp.int32, (elems, deep), 1)
    low = lax.broadcasted_iota(jnp.int32, (elems, deep), 0) * chans
    spread = jnp.where((lane >= low) & (lane < low + chans), 1.0, 0.0).astype(jnp.bfloat16)
    loads[0].wait()
    w32[...] = w16[...].astype(jnp.float32)
    by_channel = jnp.concatenate([w32[pl.ds(c, rows, stride=chans), :] for c in range(chans)])
    wide = jnp.dot(by_channel.astype(jnp.bfloat16), spread, preferred_element_type=jnp.float32)
    wide = wide.reshape(chans, rows, deep)
    lane = lax.rem(lax.broadcasted_iota(jnp.int32, wide.shape, 2), chans)
    wide = jnp.where(lane == lax.broadcasted_iota(jnp.int32, wide.shape, 0), wide, 0.0)
    wide = wide.reshape(chans * rows, deep).astype(jnp.bfloat16)
    half = rows // 2
    loads[1].wait()
    volts_both = jnp.concatenate([volts[p].reshape(deep, samples) for p in range(planes)], axis=1)
    sums = jnp.dot(wide, volts_both, preferred_element_type=jnp.float32)
    sums = sums.reshape(chans, 2, half, planes * samples)
    by_real, by_imag = sums[..., :samples], sums[..., samples:]
    both[:, 0] = by_real[:, 0] + by_imag[:, 1]
    both[:, 1] = by_imag[:, 0] - by_real[:, 1]
    owned = chans // parts
    me = lax.axis_index("elem")
    mine_ref[...] = both[pl.ds(me * owned, owned)].reshape(mine_ref.shape)
    copy_ref[...] = mine_ref[...].astype(jnp.bfloat16)
    for step in range(1, parts):
        other = lax.rem(me + step, parts) * owned
        send_ref[step - 1] = both[pl.ds(other, owned)].reshape(mine_ref.shape).astype(jnp.bfloat16)


def partial_beams(voltages, weights, parts):
    planes, _, elems, chans, samples = voltages.shape
    rows = planes * weights.shape[1]
    owned = chans // parts
    return pl.pallas_call(
        functools.partial(beam_kernel, parts),
        in_specs=[pl.BlockSpec(memory_space=pltpu.HBM)] * 2,
        out_shape=(
            jax.ShapeDtypeStruct((owned, rows, samples), jnp.float32),
            jax.ShapeDtypeStruct((owned, rows, samples), jnp.bfloat16),
            jax.ShapeDtypeStruct((parts - 1, owned, rows, samples), jnp.bfloat16),
        ),
        out_specs=[pl.BlockSpec(memory_space=pltpu.VMEM)] * 3,
        compiler_params=pltpu.CompilerParams(vmem_limit_bytes=55080 << 10),
        scratch_shapes=[
            pltpu.VMEM((rows * chans, elems), weights.dtype),
            pltpu.VMEM((rows * chans, elems), jnp.float32),
            pltpu.VMEM((planes, elems, chans, samples), voltages.dtype),
            pltpu.VMEM((chans, planes, rows // planes, samples), jnp.float32),
            pltpu.SemaphoreType.DMA((2,)),
        ],
    )(voltages[:, 0], weights.transpose(0, 1, 3, 2).reshape(rows * chans, elems))


def place_of(chip, stages):
    index, flip, size = 0, 0, 1
    for steps in stages:
        bits = [s >> 1 for s in steps if (s >> 1) & ((s >> 1) - 1) == 0]
        spots, flips = 0, 0
        for at, step in enumerate(steps):
            key = sum(1 << j for j, b in enumerate(bits) if (step >> 1) & b)
            spots |= (at + 1) << (2 * key)
            flips |= (step & 1) << key
        key = sum(((chip >> (b.bit_length() - 1)) & 1) << j for j, b in enumerate(bits))
        index = index + ((spots >> (2 * key)) & 3) * size
        flip = flip ^ ((flips >> key) & 1)
        size *= len(steps) + 1
    return index, flip


def spectra_kernel(stages, held_ref, rows_ref, out_ref):
    chips, chans, rows, samples = held_ref.shape
    half = rows // 2
    me = lax.axis_index("stn")
    places = []
    for chip in range(chips):
        index, flip = place_of((me >> 1) ^ chip, stages)
        places.append((index, ((me & 1) ^ flip) == 0))
    found = []
    for c in range(chans):
        tiles = []
        for index, held_first in places:
            held = held_ref[index, c]
            tiles += [held, held]
        tiles = [t.astype(jnp.float32) for t in tiles]
        real = jnp.concatenate([t[:half] for t in tiles])
        imag = jnp.concatenate([t[half:] for t in tiles])
        right = jnp.concatenate([real, imag], axis=1)
        own = rows_ref[0, c].astype(jnp.float32)
        left = jnp.concatenate([own, jnp.concatenate([own[half:], -own[:half]])], axis=1)
        found.append(
            lax.dot_general(
                left.astype(jnp.bfloat16), right.astype(jnp.bfloat16), (((1,), (1,)), ((), ())),
                preferred_element_type=jnp.float32,
            )
        )
    spec = jnp.concatenate(found)
    lane = lax.broadcasted_iota(jnp.int32, spec.shape, 1)
    wanted = 0
    for chip, (_, held_first) in enumerate(places):
        first = jnp.where(held_first, 2 * chip * half, (2 * chip + 1) * half)
        wanted = wanted + ((lane >= first) & (lane < first + half)).astype(jnp.int32)
    spec = jnp.where(wanted > 0, spec, 0.0).reshape(chans, 2, half, -1) / jnp.float32(samples)
    out_ref[0] = spec[:, 0]
    out_ref[1] = spec[:, 1]


def half_spectra(held, block, stages):
    chips, chans, rows, samples = held.shape
    half = rows // 2
    return pl.pallas_call(
        functools.partial(spectra_kernel, stages),
        out_shape=jax.ShapeDtypeStruct((2, chans, half, 2 * chips * half), jnp.float32),
        compiler_params=pltpu.CompilerParams(vmem_limit_bytes=room_for(held, block)),
        cost_estimate=pl.CostEstimate(
            flops=16 * held.size * half, bytes_accessed=2 * held.size, transcendentals=0
        ),
    )(held, block)


def gather_plan(stations):
    bits = []
    while stations > 2:
        stations //= 2
        bits.append(stations)
    first, rest = bits[0], bits[1:]
    stages = []
    while rest:
        pair, rest = rest[:2], rest[2:]
        stages.append([sum(pair), pair[0], pair[1] + 1] if len(pair) == 2 else [pair[0] + 1])
    return first + 1, stages


def body(stations, parts, voltages, weights):
    mine, copy, sent = partial_beams(voltages, weights, parts)
    near, stages = gather_plan(stations)
    other = lax.ppermute(copy, "stn", [(i, i ^ near) for i in range(stations)]).astype(jnp.float32)
    for step in range(1, parts):
        here = [(e, (e + step) % parts) for e in range(parts)]
        there = [(s * parts + e, (s ^ near) * parts + f) for s in range(stations) for e, f in here]
        mine = mine + lax.ppermute(sent[step - 1], "elem", here).astype(jnp.float32)
        other = other + lax.ppermute(sent[step - 1], ("stn", "elem"), there).astype(jnp.float32)
    own = mine.astype(jnp.bfloat16)[None]
    swap = [(i, i ^ 1) for i in range(stations)]
    pair = lax.ppermute(own, "stn", swap)
    held = jnp.concatenate([own, other.astype(jnp.bfloat16)[None]])
    for steps in stages:
        got = [lax.ppermute(held, "stn", [(i, i ^ step) for i in range(stations)]) for step in steps]
        held = jnp.concatenate([held] + got)
    theirs = half_spectra(held, pair, [[near]] + stages)
    return half_spectra(held, own, [[near]] + stages) + lax.ppermute(theirs, "stn", swap)


def solution(mesh):
    placed = (P(None, "stn", "elem", None, None), P(None, None, "elem", None))
    return jax.shard_map(
        functools.partial(body, mesh.shape["stn"], mesh.shape["elem"]),
        mesh=mesh, in_specs=placed, out_specs=P(None, "elem", "stn", None), check_vma=False,
    )
```

```python
import functools

import jax
import jax.numpy as jnp
from jax import lax
from jax.experimental import pallas as pl
from jax.experimental.pallas import tpu as pltpu
from jax.sharding import PartitionSpec as P


def room_for(*arrays):
    return (4 << 20) + 4 * sum(a.size * a.dtype.itemsize for a in arrays)


def beam_kernel(parts, v_ref, w_ref, mine_ref, copy_ref, send_ref, w16, w32, volts, both, sems):
    planes, elems, chans, samples = v_ref.shape
    rows = w_ref.shape[0] // chans
    deep = elems * chans
    loads = [
        pltpu.make_async_copy(w_ref, w16, sems.at[0]), pltpu.make_async_copy(v_ref, volts, sems.at[1])
    ]
    for load in loads:
        load.start()
    lane = lax.broadcasted_iota(jnp.int32, (elems, deep), 1)
    low = lax.broadcasted_iota(jnp.int32, (elems, deep), 0) * chans
    spread = jnp.where((lane >= low) & (lane < low + chans), 1.0, 0.0).astype(jnp.bfloat16)
    loads[0].wait()
    w32[...] = w16[...].astype(jnp.float32)
    by_channel = jnp.concatenate([w32[pl.ds(c, rows, stride=chans), :] for c in range(chans)])
    wide = jnp.dot(by_channel.astype(jnp.bfloat16), spread, preferred_element_type=jnp.float32)
    wide = wide.reshape(chans, rows, deep)
    lane = lax.rem(lax.broadcasted_iota(jnp.int32, wide.shape, 2), chans)
    wide = jnp.where(lane == lax.broadcasted_iota(jnp.int32, wide.shape, 0), wide, 0.0)
    wide = wide.reshape(chans * rows, deep).astype(jnp.bfloat16)
    half = rows // 2
    loads[1].wait()
    volts_both = jnp.concatenate([volts[p].reshape(deep, samples) for p in range(planes)], axis=1)
    sums = jnp.dot(wide, volts_both, preferred_element_type=jnp.float32)
    sums = sums.reshape(chans, 2, half, planes * samples)
    by_real, by_imag = sums[..., :samples], sums[..., samples:]
    both[:, 0] = by_real[:, 0] + by_imag[:, 1]
    both[:, 1] = by_imag[:, 0] - by_real[:, 1]
    owned = chans // parts
    me = lax.axis_index("elem")
    mine_ref[...] = both[pl.ds(me * owned, owned)].reshape(mine_ref.shape)
    copy_ref[...] = mine_ref[...].astype(jnp.bfloat16)
    for step in range(1, parts):
        other = lax.rem(me + step, parts) * owned
        send_ref[step - 1] = both[pl.ds(other, owned)].reshape(mine_ref.shape).astype(jnp.bfloat16)


def partial_beams(voltages, weights, parts):
    planes, _, elems, chans, samples = voltages.shape
    rows = planes * weights.shape[1]
    owned = chans // parts
    return pl.pallas_call(
        functools.partial(beam_kernel, parts),
        in_specs=[pl.BlockSpec(memory_space=pltpu.HBM)] * 2,
        out_shape=(
            jax.ShapeDtypeStruct((owned, rows, samples), jnp.float32),
            jax.ShapeDtypeStruct((owned, rows, samples), jnp.bfloat16),
            jax.ShapeDtypeStruct((parts - 1, owned, rows, samples), jnp.bfloat16),
        ),
        out_specs=[pl.BlockSpec(memory_space=pltpu.VMEM)] * 3,
        compiler_params=pltpu.CompilerParams(vmem_limit_bytes=55080 << 10),
        scratch_shapes=[
            pltpu.VMEM((rows * chans, elems), weights.dtype),
            pltpu.VMEM((rows * chans, elems), jnp.float32),
            pltpu.VMEM((planes, elems, chans, samples), voltages.dtype),
            pltpu.VMEM((chans, planes, rows // planes, samples), jnp.float32),
            pltpu.SemaphoreType.DMA((2,)),
        ],
    )(voltages[:, 0], weights.transpose(0, 1, 3, 2).reshape(rows * chans, elems))


def place_of(chip, core, stages):
    index, flip, size = 0, 0, 1
    for routes in stages:
        bits = sorted({x for route in routes for x in route[:2] if x & (x - 1) == 0})
        spots, flips = [0, 0], [0, 0]
        for at, route in enumerate(routes):
            for mine in range(2):
                key = sum(1 << j for j, b in enumerate(bits) if route[mine ^ route[2]] & b)
                spots[mine] |= (at + 1) << (2 * key)
                flips[mine] |= route[2] << key
        key = sum(((chip >> (b.bit_length() - 1)) & 1) << j for j, b in enumerate(bits))
        spot = jnp.where(core == 0, spots[0], spots[1]) if spots[0] != spots[1] else spots[0]
        index = index + ((spot >> (2 * key)) & 3) * size
        flip = flip ^ ((flips[0] >> key) & 1)
        size *= len(routes) + 1
    return index, flip


def spectra_kernel(stages, held_ref, rows_ref, out_ref):
    chips, chans, rows, samples = held_ref.shape
    half = rows // 2
    me = lax.axis_index("stn")
    places = []
    for chip in range(chips):
        index, flip = place_of((me >> 1) ^ chip, me & 1, stages)
        places.append((index, ((me & 1) ^ flip) == 0))
    found = []
    for c in range(chans):
        tiles = []
        for index, held_first in places:
            held = held_ref[index, c]
            tiles += [held, held]
        tiles = [t.astype(jnp.float32) for t in tiles]
        real = jnp.concatenate([t[:half] for t in tiles])
        imag = jnp.concatenate([t[half:] for t in tiles])
        right = jnp.concatenate([real, imag], axis=1)
        own = rows_ref[0, c].astype(jnp.float32)
        left = jnp.concatenate([own, jnp.concatenate([own[half:], -own[:half]])], axis=1)
        found.append(
            lax.dot_general(
                left.astype(jnp.bfloat16), right.astype(jnp.bfloat16), (((1,), (1,)), ((), ())),
                preferred_element_type=jnp.float32,
            )
        )
    spec = jnp.concatenate(found)
    lane = lax.broadcasted_iota(jnp.int32, spec.shape, 1)
    wanted = 0
    for chip, (_, held_first) in enumerate(places):
        first = jnp.where(held_first, 2 * chip * half, (2 * chip + 1) * half)
        wanted = wanted + ((lane >= first) & (lane < first + half)).astype(jnp.int32)
    spec = jnp.where(wanted > 0, spec, 0.0).reshape(chans, 2, half, -1) / jnp.float32(samples)
    out_ref[0] = spec[:, 0]
    out_ref[1] = spec[:, 1]


def half_spectra(held, block, stages):
    chips, chans, rows, samples = held.shape
    half = rows // 2
    return pl.pallas_call(
        functools.partial(spectra_kernel, stages),
        out_shape=jax.ShapeDtypeStruct((2, chans, half, 2 * chips * half), jnp.float32),
        compiler_params=pltpu.CompilerParams(vmem_limit_bytes=room_for(held, block)),
        cost_estimate=pl.CostEstimate(
            flops=16 * held.size * half, bytes_accessed=2 * held.size, transcendentals=0
        ),
    )(held, block)


def gather_plan(stations):
    bits = []
    while stations > 2:
        stations //= 2
        bits.append(stations // 2)
    first, rest = bits[0], bits[1:]
    stages = []
    while rest:
        pair, rest = rest[:2], rest[2:]
        if len(pair) == 2:
            low, high, both = pair[1], pair[0], sum(pair)
            stages.append([(low, both, 0), (both, low, 0), (high, high, 1)])
        else:
            stages.append([(pair[0], pair[0], 1)])
    return first, stages


def across(block, route, stations):
    pairs = [(i, i ^ (2 * route[i & 1] + route[2])) for i in range(stations)]
    return lax.ppermute(block, "stn", pairs)


def body(stations, parts, voltages, weights):
    mine, copy, sent = partial_beams(voltages, weights, parts)
    near, stages = gather_plan(stations)
    first = (near, near, 1)
    other = across(copy, first, stations).astype(jnp.float32)
    for step in range(1, parts):
        here = [(e, (e + step) % parts) for e in range(parts)]
        there = [
            (s * parts + e, (s ^ (2 * near + 1)) * parts + f) for s in range(stations) for e, f in here
        ]
        mine = mine + lax.ppermute(sent[step - 1], "elem", here).astype(jnp.float32)
        other = other + lax.ppermute(sent[step - 1], ("stn", "elem"), there).astype(jnp.float32)
    own = mine.astype(jnp.bfloat16)[None]
    pair = across(own, (0, 0, 1), stations)
    held = jnp.concatenate([own, other.astype(jnp.bfloat16)[None]])
    for routes in stages:
        held = jnp.concatenate([held] + [across(held, route, stations) for route in routes])
    theirs = half_spectra(held, pair, [[first]] + stages)
    return half_spectra(held, own, [[first]] + stages) + across(theirs, (0, 0, 1), stations)


def solution(mesh):
    placed = (P(None, "stn", "elem", None, None), P(None, None, "elem", None))
    return jax.shard_map(
        functools.partial(body, mesh.shape["stn"], mesh.shape["elem"]),
        mesh=mesh, in_specs=placed, out_specs=P(None, "elem", "stn", None), check_vma=False,
    )
```

```python
import functools

import jax
import jax.numpy as jnp
from jax import lax
from jax.experimental import pallas as pl
from jax.experimental.pallas import tpu as pltpu
from jax.sharding import PartitionSpec as P


def room_for(*arrays):
    return (4 << 20) + 4 * sum(a.size * a.dtype.itemsize for a in arrays)


def beam_kernel(parts, v_ref, w_ref, mine_ref, copy_ref, send_ref, w16, w32, volts, both, sems):
    planes, elems, chans, samples = v_ref.shape
    rows = w_ref.shape[0] // chans
    deep = elems * chans
    loads = [
        pltpu.make_async_copy(w_ref, w16, sems.at[0]), pltpu.make_async_copy(v_ref, volts, sems.at[1])
    ]
    for load in loads:
        load.start()
    lane = lax.broadcasted_iota(jnp.int32, (elems, deep), 1)
    low = lax.broadcasted_iota(jnp.int32, (elems, deep), 0) * chans
    spread = jnp.where((lane >= low) & (lane < low + chans), 1.0, 0.0).astype(jnp.bfloat16)
    loads[0].wait()
    w32[...] = w16[...].astype(jnp.float32)
    by_channel = jnp.concatenate([w32[pl.ds(c, rows, stride=chans), :] for c in range(chans)])
    wide = jnp.dot(by_channel.astype(jnp.bfloat16), spread, preferred_element_type=jnp.float32)
    wide = wide.reshape(chans, rows, deep)
    lane = lax.rem(lax.broadcasted_iota(jnp.int32, wide.shape, 2), chans)
    wide = jnp.where(lane == lax.broadcasted_iota(jnp.int32, wide.shape, 0), wide, 0.0)
    wide = wide.reshape(chans * rows, deep).astype(jnp.bfloat16)
    half = rows // 2
    loads[1].wait()
    volts_both = jnp.concatenate([volts[p].reshape(deep, samples) for p in range(planes)], axis=1)
    sums = jnp.dot(wide, volts_both, preferred_element_type=jnp.float32)
    sums = sums.reshape(chans, 2, half, planes * samples)
    by_real, by_imag = sums[..., :samples], sums[..., samples:]
    both[:, 0] = by_real[:, 0] + by_imag[:, 1]
    both[:, 1] = by_imag[:, 0] - by_real[:, 1]
    owned = chans // parts
    me = lax.axis_index("elem")
    mine_ref[...] = both[pl.ds(me * owned, owned)].reshape(mine_ref.shape)
    copy_ref[...] = mine_ref[...].astype(jnp.bfloat16)
    for step in range(1, parts):
        other = lax.rem(me + step, parts) * owned
        send_ref[step - 1] = both[pl.ds(other, owned)].reshape(mine_ref.shape).astype(jnp.bfloat16)


def partial_beams(voltages, weights, parts):
    planes, _, elems, chans, samples = voltages.shape
    rows = planes * weights.shape[1]
    owned = chans // parts
    return pl.pallas_call(
        functools.partial(beam_kernel, parts),
        in_specs=[pl.BlockSpec(memory_space=pltpu.HBM)] * 2,
        out_shape=(
            jax.ShapeDtypeStruct((owned, rows, samples), jnp.float32),
            jax.ShapeDtypeStruct((owned, rows, samples), jnp.bfloat16),
            jax.ShapeDtypeStruct((parts - 1, owned, rows, samples), jnp.bfloat16),
        ),
        out_specs=[pl.BlockSpec(memory_space=pltpu.VMEM)] * 3,
        compiler_params=pltpu.CompilerParams(vmem_limit_bytes=55080 << 10),
        scratch_shapes=[
            pltpu.VMEM((rows * chans, elems), weights.dtype),
            pltpu.VMEM((rows * chans, elems), jnp.float32),
            pltpu.VMEM((planes, elems, chans, samples), voltages.dtype),
            pltpu.VMEM((chans, planes, rows // planes, samples), jnp.float32),
            pltpu.SemaphoreType.DMA((2,)),
        ],
    )(voltages[:, 0], weights.transpose(0, 1, 3, 2).reshape(rows * chans, elems))


def place_of(chip, core, stages):
    index, flip, size = 0, 0, 1
    for routes in stages:
        bits = sorted({x for route in routes for x in route[:2] if x & (x - 1) == 0})
        spots, flips = [0, 0], [0, 0]
        for at, route in enumerate(routes):
            for mine in range(2):
                key = sum(1 << j for j, b in enumerate(bits) if route[mine ^ route[2]] & b)
                spots[mine] |= (at + 1) << (2 * key)
                flips[mine] |= route[2] << key
        key = sum(((chip >> (b.bit_length() - 1)) & 1) << j for j, b in enumerate(bits))
        spot = jnp.where(core == 0, spots[0], spots[1]) if spots[0] != spots[1] else spots[0]
        index = index + ((spot >> (2 * key)) & 3) * size
        flip = flip ^ ((flips[0] >> key) & 1)
        size *= len(routes) + 1
    return index, flip


def spectra_kernel(stages, held_ref, rows_ref, out_ref):
    chips, chans, rows, samples = held_ref.shape
    half = rows // 2
    me = lax.axis_index("stn")
    places = []
    for chip in range(chips):
        index, flip = place_of((me >> 1) ^ chip, me & 1, stages)
        places.append((index, ((me & 1) ^ flip) == 0))
    found = []
    for c in range(chans):
        tiles = []
        for index, held_first in places:
            held = held_ref[index, c]
            tiles += [held, held]
        tiles = [t.astype(jnp.float32) for t in tiles]
        real = jnp.concatenate([t[:half] for t in tiles])
        imag = jnp.concatenate([t[half:] for t in tiles])
        right = jnp.concatenate([real, imag], axis=1)
        own = rows_ref[0, c].astype(jnp.float32)
        left = jnp.concatenate([own, jnp.concatenate([own[half:], -own[:half]])], axis=1)
        found.append(
            lax.dot_general(
                left.astype(jnp.bfloat16), right.astype(jnp.bfloat16), (((1,), (1,)), ((), ())),
                preferred_element_type=jnp.float32,
            )
        )
    spec = jnp.concatenate(found)
    lane = lax.broadcasted_iota(jnp.int32, (1, spec.shape[1]), 1)
    scale = jnp.zeros(lane.shape, jnp.float32)
    for chip, (_, held_first) in enumerate(places):
        first = jnp.where(held_first, 2 * chip * half, (2 * chip + 1) * half)
        scale = jnp.where((lane >= first) & (lane < first + half), 1.0, scale)
    spec = (spec * scale).reshape(chans, 2, half, -1) / jnp.float32(samples)
    out_ref[0] = spec[:, 0]
    out_ref[1] = spec[:, 1]


def half_spectra(held, block, stages):
    chips, chans, rows, samples = held.shape
    half = rows // 2
    return pl.pallas_call(
        functools.partial(spectra_kernel, stages),
        out_shape=jax.ShapeDtypeStruct((2, chans, half, 2 * chips * half), jnp.float32),
        compiler_params=pltpu.CompilerParams(vmem_limit_bytes=room_for(held, block)),
        cost_estimate=pl.CostEstimate(
            flops=16 * held.size * half, bytes_accessed=2 * held.size, transcendentals=0
        ),
    )(held, block)


def gather_plan(stations):
    bits = []
    while stations > 2:
        stations //= 2
        bits.append(stations // 2)
    first, rest = bits[0], bits[1:]
    stages = []
    while rest:
        pair, rest = rest[:2], rest[2:]
        if len(pair) == 2:
            low, high, both = pair[1], pair[0], sum(pair)
            stages.append([(low, both, 0), (both, low, 0), (high, high, 1)])
        else:
            stages.append([(pair[0], pair[0], 1)])
    return first, stages


def across(block, route, stations):
    pairs = [(i, i ^ (2 * route[i & 1] + route[2])) for i in range(stations)]
    return lax.ppermute(block, "stn", pairs)


def body(stations, parts, voltages, weights):
    mine, copy, sent = partial_beams(voltages, weights, parts)
    near, stages = gather_plan(stations)
    first = (near, near, 1)
    other = across(copy, first, stations).astype(jnp.float32)
    for step in range(1, parts):
        here = [(e, (e + step) % parts) for e in range(parts)]
        there = [
            (s * parts + e, (s ^ (2 * near + 1)) * parts + f) for s in range(stations) for e, f in here
        ]
        mine = mine + lax.ppermute(sent[step - 1], "elem", here).astype(jnp.float32)
        other = other + lax.ppermute(sent[step - 1], ("stn", "elem"), there).astype(jnp.float32)
    own = mine.astype(jnp.bfloat16)[None]
    pair = across(own, (0, 0, 1), stations)
    held = jnp.concatenate([own, other.astype(jnp.bfloat16)[None]])
    for routes in stages:
        held = jnp.concatenate([held] + [across(held, route, stations) for route in routes])
    theirs = half_spectra(held, pair, [[first]] + stages)
    return half_spectra(held, own, [[first]] + stages) + across(theirs, (0, 0, 1), stations)


def solution(mesh):
    placed = (P(None, "stn", "elem", None, None), P(None, None, "elem", None))
    return jax.shard_map(
        functools.partial(body, mesh.shape["stn"], mesh.shape["elem"]),
        mesh=mesh, in_specs=placed, out_specs=P(None, "elem", "stn", None), check_vma=False,
    )
```

```python
import functools

import jax
import jax.numpy as jnp
from jax import lax
from jax.experimental import pallas as pl
from jax.experimental.pallas import tpu as pltpu
from jax.sharding import PartitionSpec as P


def room_for(*arrays):
    return (4 << 20) + 4 * sum(a.size * a.dtype.itemsize for a in arrays)


def beam_kernel(parts, v_ref, w_ref, mine_ref, copy_ref, send_ref, w16, w32, volts, both, sems):
    planes, elems, chans, samples = v_ref.shape
    rows = w_ref.shape[0] // chans
    deep = elems * chans
    loads = [
        pltpu.make_async_copy(w_ref, w16, sems.at[0]), pltpu.make_async_copy(v_ref, volts, sems.at[1])
    ]
    for load in loads:
        load.start()
    lane = lax.broadcasted_iota(jnp.int32, (elems, deep), 1)
    low = lax.broadcasted_iota(jnp.int32, (elems, deep), 0) * chans
    spread = jnp.where((lane >= low) & (lane < low + chans), 1.0, 0.0).astype(jnp.bfloat16)
    loads[0].wait()
    w32[...] = w16[...].astype(jnp.float32)
    by_channel = jnp.concatenate([w32[pl.ds(c, rows, stride=chans), :] for c in range(chans)])
    wide = jnp.dot(by_channel.astype(jnp.bfloat16), spread, preferred_element_type=jnp.float32)
    wide = wide.reshape(chans, rows, deep)
    lane = lax.rem(lax.broadcasted_iota(jnp.int32, wide.shape, 2), chans)
    wide = jnp.where(lane == lax.broadcasted_iota(jnp.int32, wide.shape, 0), wide, 0.0)
    wide = wide.reshape(chans * rows, deep).astype(jnp.bfloat16)
    half = rows // 2
    loads[1].wait()
    volts_both = jnp.concatenate([volts[p].reshape(deep, samples) for p in range(planes)], axis=1)
    sums = jnp.dot(wide, volts_both, preferred_element_type=jnp.float32)
    sums = sums.reshape(chans, 2, half, planes * samples)
    by_real, by_imag = sums[..., :samples], sums[..., samples:]
    both[:, 0] = by_real[:, 0] + by_imag[:, 1]
    both[:, 1] = by_imag[:, 0] - by_real[:, 1]
    owned = chans // parts
    me = lax.axis_index("elem")
    mine_ref[...] = both[pl.ds(me * owned, owned)].reshape(mine_ref.shape)
    copy_ref[...] = mine_ref[...].astype(jnp.bfloat16)
    for step in range(1, parts):
        other = lax.rem(me + step, parts) * owned
        send_ref[step - 1] = both[pl.ds(other, owned)].reshape(mine_ref.shape).astype(jnp.bfloat16)


def partial_beams(voltages, weights, parts):
    planes, _, elems, chans, samples = voltages.shape
    rows = planes * weights.shape[1]
    owned = chans // parts
    return pl.pallas_call(
        functools.partial(beam_kernel, parts),
        in_specs=[pl.BlockSpec(memory_space=pltpu.HBM)] * 2,
        out_shape=(
            jax.ShapeDtypeStruct((owned, rows, samples), jnp.float32),
            jax.ShapeDtypeStruct((owned, rows, samples), jnp.bfloat16),
            jax.ShapeDtypeStruct((parts - 1, owned, rows, samples), jnp.bfloat16),
        ),
        out_specs=[pl.BlockSpec(memory_space=pltpu.VMEM)] * 3,
        compiler_params=pltpu.CompilerParams(vmem_limit_bytes=55080 << 10),
        scratch_shapes=[
            pltpu.VMEM((rows * chans, elems), weights.dtype),
            pltpu.VMEM((rows * chans, elems), jnp.float32),
            pltpu.VMEM((planes, elems, chans, samples), voltages.dtype),
            pltpu.VMEM((chans, planes, rows // planes, samples), jnp.float32),
            pltpu.SemaphoreType.DMA((2,)),
        ],
    )(voltages[:, 0], weights.transpose(0, 1, 3, 2).reshape(rows * chans, elems))


def place_of(chip, core, stages):
    index, flip, size = 0, 0, 1
    for routes in stages:
        bits = sorted({x for route in routes for x in route[:2] if x & (x - 1) == 0})
        low, mask = bits[0].bit_length() - 1, 2 ** len(bits) - 1
        codes = [0, 0]
        for at, route in enumerate(routes):
            for mine in range(2):
                key = (route[mine ^ route[2]] >> low) & mask
                codes[mine] |= (4 * route[2] + at + 1) << (4 * key)
        code = jnp.where(core == 0, codes[0], codes[1]) if codes[0] != codes[1] else codes[0]
        code = (code >> (4 * ((chip >> low) & mask))) & 7
        index = index + (code & 3) * size
        flip = flip ^ (code >> 2)
        size *= len(routes) + 1
    return index, flip


def spectra_kernel(stages, held_ref, rows_ref, out_ref):
    chips, chans, rows, samples = held_ref.shape
    half = rows // 2
    me = lax.axis_index("stn")
    places = []
    for chip in range(chips):
        index, flip = place_of((me >> 1) ^ chip, me & 1, stages)
        places.append((index, ((me & 1) ^ flip) == 0))
    found = []
    for c in range(chans):
        tiles = []
        for index, held_first in places:
            held = held_ref[index, c]
            tiles += [held, held]
        tiles = [t.astype(jnp.float32) for t in tiles]
        real = jnp.concatenate([t[:half] for t in tiles])
        imag = jnp.concatenate([t[half:] for t in tiles])
        right = jnp.concatenate([real, imag], axis=1)
        own = rows_ref[0, c].astype(jnp.float32)
        left = jnp.concatenate([own, jnp.concatenate([own[half:], -own[:half]])], axis=1)
        found.append(
            lax.dot_general(
                left.astype(jnp.bfloat16), right.astype(jnp.bfloat16), (((1,), (1,)), ((), ())),
                preferred_element_type=jnp.float32,
            )
        )
    spec = jnp.concatenate(found)
    lane = lax.broadcasted_iota(jnp.int32, (1, spec.shape[1]), 1)
    scale = jnp.zeros(lane.shape, jnp.float32)
    for chip, (_, held_first) in enumerate(places):
        first = jnp.where(held_first, 2 * chip * half, (2 * chip + 1) * half)
        scale = jnp.where((lane >= first) & (lane < first + half), 1.0, scale)
    spec = (spec * scale).reshape(chans, 2, half, -1) / jnp.float32(samples)
    out_ref[0] = spec[:, 0]
    out_ref[1] = spec[:, 1]


def half_spectra(held, block, stages):
    chips, chans, rows, samples = held.shape
    half = rows // 2
    return pl.pallas_call(
        functools.partial(spectra_kernel, stages),
        out_shape=jax.ShapeDtypeStruct((2, chans, half, 2 * chips * half), jnp.float32),
        compiler_params=pltpu.CompilerParams(vmem_limit_bytes=room_for(held, block)),
        cost_estimate=pl.CostEstimate(
            flops=16 * held.size * half, bytes_accessed=2 * held.size, transcendentals=0
        ),
    )(held, block)


def gather_plan(stations):
    bits = []
    while stations > 2:
        stations //= 2
        bits.append(stations // 2)
    first, rest = bits[0], bits[1:]
    stages = []
    while rest:
        pair, rest = rest[:2], rest[2:]
        if len(pair) == 2:
            low, high, both = pair[1], pair[0], sum(pair)
            stages.append([(low, both, 0), (both, low, 0), (high, high, 1)])
        else:
            stages.append([(pair[0], pair[0], 1)])
    return first, stages


def across(block, route, stations):
    pairs = [(i, i ^ (2 * route[i & 1] + route[2])) for i in range(stations)]
    return lax.ppermute(block, "stn", pairs)


def body(stations, parts, voltages, weights):
    mine, copy, sent = partial_beams(voltages, weights, parts)
    near, stages = gather_plan(stations)
    first = (near, near, 1)
    other = across(copy, first, stations).astype(jnp.float32)
    for step in range(1, parts):
        here = [(e, (e + step) % parts) for e in range(parts)]
        there = [
            (s * parts + e, (s ^ (2 * near + 1)) * parts + f) for s in range(stations) for e, f in here
        ]
        mine = mine + lax.ppermute(sent[step - 1], "elem", here).astype(jnp.float32)
        other = other + lax.ppermute(sent[step - 1], ("stn", "elem"), there).astype(jnp.float32)
    own = mine.astype(jnp.bfloat16)[None]
    pair = across(own, (0, 0, 1), stations)
    held = jnp.concatenate([own, other.astype(jnp.bfloat16)[None]])
    for routes in stages:
        held = jnp.concatenate([held] + [across(held, route, stations) for route in routes])
    theirs = half_spectra(held, pair, [[first]] + stages)
    return half_spectra(held, own, [[first]] + stages) + across(theirs, (0, 0, 1), stations)


def solution(mesh):
    placed = (P(None, "stn", "elem", None, None), P(None, None, "elem", None))
    return jax.shard_map(
        functools.partial(body, mesh.shape["stn"], mesh.shape["elem"]),
        mesh=mesh, in_specs=placed, out_specs=P(None, "elem", "stn", None), check_vma=False,
    )
```
